32 devices in a mesh: rep: 2 (over x), gx: 4 (over y, core), gy: 4 (over z).
Axes of the slice: x: 2, y: 2, z: 4, core: 2. Of those that a mesh axis runs over, the one named last changes fastest.
Arguments:
- tokens: bfloat16 [4096, 2048], P(('rep', 'gx', 'gy')), parts along dimension 0, may hold values from -6 to 6
- grad_out: bfloat16 [4096, 2048], P(('rep', 'gx', 'gy')), parts along dimension 0, may hold values from -6 to 6
- route_ids: int32 [4096, 10], P(('rep', 'gx', 'gy')), parts along dimension 0, may hold values from 0 to 31, all different within a row; in each aligned block of 128 rows (0 to 127, 128 to 255, ...) at most 50 rows name the same one
- gate_weights: float32 [4096, 10], P(('rep', 'gx', 'gy')), parts along dimension 0, may hold values from 0.05 to 0.5
- w_gate: bfloat16 [32, 2048, 256], P(('gx', 'gy')), may hold values from -0.125 to 0.125
- w_up: bfloat16 [32, 2048, 256], P(('gx', 'gy')), may hold values from -0.125 to 0.125
- w_down: bfloat16 [32, 256, 2048], P(('gx', 'gy')), may hold values from -0.375 to 0.375
Outputs:
- grad_tokens: bfloat16 [4096, 2048], P(('rep', 'gx', 'gy')), parts along dimension 0
- grad_down: bfloat16 [64, 256, 2048], P(('rep', 'gx', 'gy')), parts along dimension 0
The draws below stay inside these ranges and needn't reach their ends.
There are 2 independent parts, one for each index of `rep`. The reference program is written for one: setup_inputs(seed, part) draws one part's arguments, and reference() takes and returns one part's arrays. A program takes and returns all parts, laid end to end along the dimension named above; an argument that names none is the same for every part. Nothing has to cross between parts.
Inputs may be any that keep to these rules, and one draw needn't show every extreme that they name: `route_ids`: each row names 10 different experts. Among the 128 rows of one device no expert is named by more than 50 rows, and in some aligned block of 128 rows some expert is named by exactly 50 rows.
All inputs are finite; a program needn't handle non-finite values.
Results may differ from the reference program's by a relative error of at most 0.0064.
Values may be sent and summed in bfloat16 or wider, within the bound.
A program may use at most 128 MiB of HBM per device.

```python
import math
import jax
import jax.numpy as jnp
import numpy as np
from jax import lax

D = 2048
FF = 256
TOP = 10
TOK_DEV = 128
EXPERTS = 32
TOKENS = 2048
CAP = 50
N_GX = 4
N_GY = 4


def block_levels(key, dims, pieces, smallest, top_value):
    gain, own = 1.0, jax.random.fold_in(key, 6)
    for dim, blocks in pieces:
        heights = jnp.exp(jax.random.uniform(jax.random.fold_in(own, dim), (blocks,), jnp.float32, smallest / len(pieces), top_value / len(pieces)))
        gain = gain * jnp.repeat(heights, dims[dim] // blocks).reshape([-1 if axis == dim else 1 for axis in range(len(dims))])
    return gain


def routed_block(rng, own, number, rows, amount, top, most, skew):
    sequence = jax.random.permutation(rng, amount)
    packed, ordinary = load_shares(amount, rows * top, most, skew, True), load_shares(amount, rows * top, most, skew, False)
    places = jnp.arange(amount)

    def named(sizes, offset_by):
        used = int((sizes > 0).sum())
        fixed = max(1, used // 4)
        shifted = fixed + (places - fixed + offset_by * (used - fixed)) % max(1, amount - fixed)
        return jnp.zeros((amount,), jnp.int32).at[sequence[jnp.where(places < fixed, places, shifted)]].set(jnp.asarray(sizes, jnp.int32))

    sizes = jnp.where(number % 4 == 0, named(packed, number // 4), named(ordinary, number - number // 4 - 1))
    mixed = jax.random.permutation(jax.random.fold_in(own, 3), amount)
    source_of, receiver = mixed[0:amount // 2 * 2:2], mixed[1:amount // 2 * 2:2]
    margin = jnp.minimum(sizes[source_of] - 1, most - sizes[receiver]) // 2
    margin = jnp.where((source_of == sequence[0]) | (receiver == sequence[0]) | (sizes[receiver] == 0), 0, jnp.maximum(margin, 0))
    shifted = jax.random.randint(jax.random.fold_in(own, 4), (amount // 2,), 0, 1 << 20) % (margin + 1)
    sizes = sizes.at[source_of].add(-shifted).at[receiver].add(shifted)
    labels = jnp.searchsorted(jnp.cumsum(sizes), jnp.arange(rows * top), side="right").astype(jnp.int32)
    listing = labels.reshape(top, rows).T
    listing = listing[jax.random.permutation(jax.random.fold_in(own, 1), rows)]
    offset_by = jax.random.randint(jax.random.fold_in(own, 2), (rows, 1), 0, top)
    return jnp.take_along_axis(listing, (jnp.arange(top)[None, :] + offset_by) % top, axis=1)


def load_shares(amount, total, most, lean, full):
    weights = [(1 << 20) // math.isqrt(standing ** lean) + 1 for standing in range(1, amount + 1)]
    largest = most if full else min(most, max(-(-total // amount), total * weights[0] // sum(weights)))
    least = 1 if total - largest >= amount - 1 else 0
    given, spare = [largest] + [least] * (amount - 1), total - largest - least * (amount - 1)
    while spare > 0:
        movable = [i for i in range(1, amount) if given[i] < largest] or [i for i in range(1, amount) if given[i] < most]
        whole, budget = sum([weights[i] for i in movable]), spare
        for i in movable:
            addition = min(most - given[i], max(1, budget * weights[i] // whole), spare)
            given[i] = given[i] + addition
            spare = spare - addition
    return np.array(given)


def normal_values(own_key, dims, width, bound, split=(), kind=jnp.bfloat16):
    array = width * jax.random.normal(own_key, dims, jnp.float32)
    if split:
        array = array * block_levels(own_key, dims, split, -0.22, 0.18)
    return jnp.clip(array, -bound, bound).astype(kind)


def setup_inputs(seed: int = 0, part: int = 0) -> dict:
    streams_of = jax.random.split(jax.random.key(seed), 8)
    part_splits = jax.random.split(jax.random.fold_in(streams_of[7], part), 8)
    tokens = normal_values(part_splits[0], (TOKENS, D), 1.0, 6.0, ((0, 16),))
    grad_out = normal_values(part_splits[1], (TOKENS, D), 1.0, 6.0, ((0, 16),))
    route_ids_keys = jax.random.split(jax.random.fold_in(part_splits[2], 1), TOKENS // TOK_DEV)
    route_ids_turns = jax.random.permutation(jax.random.fold_in(part_splits[2], 3), TOKENS // TOK_DEV)
    route_ids = jax.vmap(lambda own, number: routed_block(jax.random.fold_in(part_splits[2], 2), own, number, TOK_DEV, EXPERTS, TOP, CAP, 2))(route_ids_keys, route_ids_turns).reshape((TOKENS, TOP))
    gate_weights = jnp.clip(jnp.exp(math.log(0.5) - 2.3025851 * jax.random.uniform(part_splits[3], (TOKENS, TOP), jnp.float32) ** block_levels(part_splits[3], (TOKENS, TOP), ((0, 16),), -0.2, 0.2)), 0.05, 0.5)
    w_gate = normal_values(streams_of[4], (EXPERTS, D, FF), D ** -0.5, 0.125, ((0, 16),))
    w_up = normal_values(streams_of[5], (EXPERTS, D, FF), D ** -0.5, 0.125, ((0, 16),))
    w_down = normal_values(streams_of[6], (EXPERTS, FF, D), FF ** -0.5, 0.375, ((0, 16),))
    return dict(tokens=tokens, grad_out=grad_out, route_ids=route_ids, gate_weights=gate_weights, w_gate=w_gate, w_up=w_up, w_down=w_down)


def reference(tokens, grad_out, route_ids, gate_weights, w_gate, w_up, w_down):
    flat_ids = route_ids.reshape(-1).astype(jnp.int32)
    flat_gates = gate_weights.reshape(-1)
    limit = N_GX * N_GY * CAP

    def per_expert(total, expert):
        match = flat_ids == expert
        hits = jnp.nonzero(match, size=limit, fill_value=0)[0].astype(jnp.int32)
        count = jnp.sum(match.astype(jnp.int32))
        valid = jnp.arange(limit, dtype=jnp.int32) < count
        rows = (hits // TOP).astype(jnp.int32)
        inputs = jnp.where(valid[:, None], tokens[rows], jnp.zeros((), jnp.bfloat16))
        gates = jnp.where(valid, flat_gates[hits], jnp.zeros((), flat_gates.dtype))
        routed = (gates[:, None] * grad_out[rows].astype(jnp.float32)).astype(jnp.bfloat16)
        gate_mat = w_gate[expert]
        up_mat = w_up[expert]
        down_mat = w_down[expert]
        pre_gate = jnp.dot(inputs, gate_mat, preferred_element_type=jnp.float32)
        pre_up = jnp.dot(inputs, up_mat, preferred_element_type=jnp.float32)
        sigma = jax.nn.sigmoid(pre_gate)
        silu_val = pre_gate * sigma
        hidden = (silu_val * pre_up).astype(jnp.bfloat16)
        grad_hidden = jnp.dot(routed, down_mat.T, preferred_element_type=jnp.float32)
        grad_first = (grad_hidden * pre_up * sigma * (1.0 + pre_gate * (1.0 - sigma))).astype(jnp.bfloat16)
        grad_second = (grad_hidden * silu_val).astype(jnp.bfloat16)
        grad_route = (jnp.dot(grad_first, gate_mat.T, preferred_element_type=jnp.float32)
                      + jnp.dot(grad_second, up_mat.T, preferred_element_type=jnp.float32)).astype(jnp.bfloat16)
        total = total.at[rows].add(jnp.where(valid[:, None], grad_route.astype(jnp.float32), jnp.zeros((), jnp.float32)))
        grad_expert = jnp.dot(hidden.T, routed, preferred_element_type=jnp.float32).astype(jnp.bfloat16)
        return total, grad_expert

    start = jnp.zeros((TOKENS, D), jnp.float32)
    total, grad_down = lax.scan(per_expert, start, jnp.arange(EXPERTS, dtype=jnp.int32))
    return total.astype(jnp.bfloat16), grad_down
```

```python
import jax
import jax.numpy as jnp
from jax import lax
from jax.sharding import PartitionSpec as P


def routed_shards(tokens, grad_out, route_ids, gate_weights, w_gate, w_up, w_down):
    token_count = tokens.shape[0]
    model_width = tokens.shape[1]
    fanout = route_ids.shape[1]
    local_experts = w_gate.shape[0]
    outer_size = lax.axis_size("gx")
    inner_size = lax.axis_size("gy")
    devices = outer_size * inner_size
    experts = local_experts * devices
    capacity = max(2, 5 * token_count * fanout // (4 * experts))
    flat_ids = route_ids.reshape(-1)
    onehot = (flat_ids[:, None] == jnp.arange(experts, dtype=jnp.int32)[None, :]).astype(jnp.int32)
    earlier = jnp.cumsum(onehot, axis=0) - onehot
    slot_index = jnp.sum(earlier * onehot, axis=1)
    target = flat_ids // local_experts
    within = flat_ids % local_experts
    position = (within * devices + target) * capacity + slot_index
    source_rows = jnp.repeat(tokens, fanout, axis=0)
    scaled = (gate_weights.reshape(-1, 1) * jnp.repeat(grad_out, fanout, axis=0)).astype(
        jnp.bfloat16
    )
    buffer_rows = local_experts * devices * capacity
    send_inputs = jnp.zeros((buffer_rows, model_width), jnp.bfloat16).at[position].set(source_rows)
    send_grads = jnp.zeros((buffer_rows, model_width), jnp.bfloat16).at[position].set(scaled)
    flat_shape = (local_experts, devices, capacity, model_width)
    got_inputs, got_grads = (
        lax.all_to_all(
            send_inputs.reshape(flat_shape), ("gx", "gy"), split_axis=1, concat_axis=1, tiled=True
        ),
        lax.all_to_all(
            send_grads.reshape(flat_shape), ("gx", "gy"), split_axis=1, concat_axis=1, tiled=True
        ),
    )
    expert_rows = devices * capacity
    inputs = got_inputs.reshape(local_experts, expert_rows, model_width)
    routed = got_grads.reshape(local_experts, expert_rows, model_width)
    pre_gate = jnp.einsum("emd,edf->emf", inputs, w_gate, preferred_element_type=jnp.float32)
    pre_up = jnp.einsum("emd,edf->emf", inputs, w_up, preferred_element_type=jnp.float32)
    sigma = jax.nn.sigmoid(pre_gate)
    silu_val = pre_gate * sigma
    hidden = (silu_val * pre_up).astype(jnp.bfloat16)
    grad_hidden = jnp.einsum("emd,efd->emf", routed, w_down, preferred_element_type=jnp.float32)
    grad_first = (grad_hidden * pre_up * sigma * (1.0 + pre_gate * (1.0 - sigma))).astype(
        jnp.bfloat16
    )
    grad_second = (grad_hidden * silu_val).astype(jnp.bfloat16)
    grad_route = (
        jnp.einsum("emf,edf->emd", grad_first, w_gate, preferred_element_type=jnp.float32)
        + jnp.einsum("emf,edf->emd", grad_second, w_up, preferred_element_type=jnp.float32)
    ).astype(jnp.bfloat16)
    grad_down = jnp.einsum(
        "emf,emd->efd", hidden, routed, preferred_element_type=jnp.float32
    ).astype(jnp.bfloat16)
    returned = lax.all_to_all(
        grad_route.reshape(flat_shape), ("gx", "gy"), split_axis=1, concat_axis=1, tiled=True
    )
    picked = returned.reshape(buffer_rows, model_width)[position]
    grad_tokens = jnp.sum(
        picked.astype(jnp.float32).reshape(token_count, fanout, model_width), axis=1
    ).astype(jnp.bfloat16)
    return (grad_tokens, grad_down)


def gathered_shards(tokens, grad_out, route_ids, gate_weights, w_gate, w_up, w_down):
    axes = ("gx", "gy")
    local_experts = w_gate.shape[0]
    devices = lax.axis_size("gx") * lax.axis_size("gy")
    experts = local_experts * devices
    chosen = route_ids[:, :, None] == jnp.arange(experts, dtype=jnp.int32)
    dense = jnp.sum(jnp.where(chosen, gate_weights[:, :, None], 0.0), axis=1)
    all_gates = lax.all_gather(dense, axes, axis=0, tiled=True)
    inputs = lax.all_gather(tokens, axes, axis=0, tiled=True)
    grads = lax.all_gather(grad_out, axes, axis=0, tiled=True)
    me = lax.axis_index("gx") * lax.axis_size("gy") + lax.axis_index("gy")
    gates = lax.dynamic_slice_in_dim(all_gates, me * local_experts, local_experts, axis=1)
    total = 0.0
    downs = []
    for e in range(local_experts):
        routed = (gates[:, e : e + 1] * grads).astype(jnp.bfloat16)
        pre_gate = jnp.dot(inputs, w_gate[e], preferred_element_type=jnp.float32)
        pre_up = jnp.dot(inputs, w_up[e], preferred_element_type=jnp.float32)
        sigma = jax.nn.sigmoid(pre_gate)
        silu_val = pre_gate * sigma
        hidden = (silu_val * pre_up).astype(jnp.bfloat16)
        grad_hidden = jnp.dot(routed, w_down[e].T, preferred_element_type=jnp.float32)
        first = grad_hidden * pre_up * sigma * (1.0 + pre_gate * (1.0 - sigma))
        second = grad_hidden * silu_val
        total = total + jnp.dot(
            first.astype(jnp.bfloat16), w_gate[e].T, preferred_element_type=jnp.float32
        )
        total = total + jnp.dot(
            second.astype(jnp.bfloat16), w_up[e].T, preferred_element_type=jnp.float32
        )
        downs.append(
            jnp.dot(hidden.T, routed, preferred_element_type=jnp.float32).astype(jnp.bfloat16)
        )
    grad_tokens = lax.psum_scatter(
        total.astype(jnp.bfloat16), axes, scatter_dimension=0, tiled=True
    )
    return (grad_tokens, jnp.stack(downs))


def shards(*args):
    route_ids, w_gate = args[2], args[4]
    experts = w_gate.shape[0] * lax.axis_size("gx") * lax.axis_size("gy")
    if experts <= 4 * route_ids.shape[1]:
        return gathered_shards(*args)
    return routed_shards(*args)


def solution(mesh):
    placed = (
        P(("rep", "gx", "gy"), None),
        P(("rep", "gx", "gy"), None),
        P(("rep", "gx", "gy"), None),
        P(("rep", "gx", "gy"), None),
        P(("gx", "gy"), None, None),
        P(("gx", "gy"), None, None),
        P(("gx", "gy"), None, None),
    )
    return jax.shard_map(
        shards,
        mesh=mesh,
        in_specs=placed,
        out_specs=(P(("rep", "gx", "gy"), None), P(("rep", "gx", "gy"), None, None)),
        check_vma=False,
    )
```

```python
import jax
import jax.numpy as jnp
from jax import lax
from jax.experimental import pallas as pl
from jax.experimental.pallas import tpu as pltpu
from jax.sharding import PartitionSpec as P


LINE = 4
TILE = 512


def routed_shards(tokens, grad_out, route_ids, gate_weights, w_gate, w_up, w_down):
    token_count = tokens.shape[0]
    model_width = tokens.shape[1]
    fanout = route_ids.shape[1]
    local_experts = w_gate.shape[0]
    outer_size = lax.axis_size("gx")
    inner_size = lax.axis_size("gy")
    devices = outer_size * inner_size
    experts = local_experts * devices
    capacity = max(2, 5 * token_count * fanout // (4 * experts))
    flat_ids = route_ids.reshape(-1)
    onehot = (flat_ids[:, None] == jnp.arange(experts, dtype=jnp.int32)[None, :]).astype(jnp.int32)
    earlier = jnp.cumsum(onehot, axis=0) - onehot
    slot_index = jnp.sum(earlier * onehot, axis=1)
    target = flat_ids // local_experts
    within = flat_ids % local_experts
    position = (within * devices + target) * capacity + slot_index
    source_rows = jnp.repeat(tokens, fanout, axis=0)
    scaled = (gate_weights.reshape(-1, 1) * jnp.repeat(grad_out, fanout, axis=0)).astype(
        jnp.bfloat16
    )
    buffer_rows = local_experts * devices * capacity
    send_inputs = jnp.zeros((buffer_rows, model_width), jnp.bfloat16).at[position].set(source_rows)
    send_grads = jnp.zeros((buffer_rows, model_width), jnp.bfloat16).at[position].set(scaled)
    flat_shape = (local_experts, devices, capacity, model_width)
    got_inputs, got_grads = (
        lax.all_to_all(
            send_inputs.reshape(flat_shape), ("gx", "gy"), split_axis=1, concat_axis=1, tiled=True
        ),
        lax.all_to_all(
            send_grads.reshape(flat_shape), ("gx", "gy"), split_axis=1, concat_axis=1, tiled=True
        ),
    )
    expert_rows = devices * capacity
    inputs = got_inputs.reshape(local_experts, expert_rows, model_width)
    routed = got_grads.reshape(local_experts, expert_rows, model_width)
    pre_gate = jnp.einsum("emd,edf->emf", inputs, w_gate, preferred_element_type=jnp.float32)
    pre_up = jnp.einsum("emd,edf->emf", inputs, w_up, preferred_element_type=jnp.float32)
    sigma = jax.nn.sigmoid(pre_gate)
    silu_val = pre_gate * sigma
    hidden = (silu_val * pre_up).astype(jnp.bfloat16)
    grad_hidden = jnp.einsum("emd,efd->emf", routed, w_down, preferred_element_type=jnp.float32)
    grad_first = (grad_hidden * pre_up * sigma * (1.0 + pre_gate * (1.0 - sigma))).astype(
        jnp.bfloat16
    )
    grad_second = (grad_hidden * silu_val).astype(jnp.bfloat16)
    grad_route = (
        jnp.einsum("emf,edf->emd", grad_first, w_gate, preferred_element_type=jnp.float32)
        + jnp.einsum("emf,edf->emd", grad_second, w_up, preferred_element_type=jnp.float32)
    ).astype(jnp.bfloat16)
    grad_down = jnp.einsum(
        "emf,emd->efd", hidden, routed, preferred_element_type=jnp.float32
    ).astype(jnp.bfloat16)
    returned = lax.all_to_all(
        grad_route.reshape(flat_shape), ("gx", "gy"), split_axis=1, concat_axis=1, tiled=True
    )
    picked = returned.reshape(buffer_rows, model_width)[position]
    grad_tokens = jnp.sum(
        picked.astype(jnp.float32).reshape(token_count, fanout, model_width), axis=1
    ).astype(jnp.bfloat16)
    return (grad_tokens, grad_down)


def fused_kernel(
    tok_in, grd_in, gat_in, wg_in, wu_in, wd_in, gt_out, gd_out,
    tok, grd, gat, wg, wu, wd, part, core_in, y_in, z_in, down, g_first, g_second, hid, acc,
    local_sem, w_sem, send_sem, recv_sem, a_send, a_recv, b_send, b_recv, c_send, c_recv,
):
    gx, z = lax.axis_index("gx"), lax.axis_index("gy")
    y, c = gx // 2, gx % 2
    me = gx * LINE + z
    nbr = (
        {"gx": gx, "gy": z + 1},
        {"gx": gx, "gy": z - 1},
        {"gx": (1 - y) * 2 + c, "gy": z},
        {"gx": y * 2 + 1 - c, "gy": z},
    )
    bufs = (tok, grd, gat)
    own = y * LINE + z
    high = z // 2
    edge = z + high * (3 - 2 * z)

    def place(r):
        o = r + edge * (1 - r // 2) * (1 - 2 * (r % 2))
        return o + high * (3 - 2 * o)

    def hop(k, u, cc, d):
        return pltpu.make_async_remote_copy(
            src_ref=bufs[k].at[u, cc],
            dst_ref=bufs[k].at[u, cc],
            send_sem=send_sem.at[k, u, d],
            recv_sem=recv_sem.at[k, u, cc],
            device_id=nbr[d],
            device_id_type=pl.DeviceIdType.MESH,
        )

    def each_hop(k, zu, act):
        u = y * LINE + zu

        @pl.when((zu <= z) & (z < LINE - 1))
        def _():
            act(hop(k, u, c, 0))

        @pl.when((zu >= z) & (z > 0))
        def _():
            act(hop(k, u, c, 1))

        act(hop(k, u, c, 2))
        act(hop(k, u, c, 3))

    def start(copy):
        copy.start()

    def done(copy):
        copy.wait_send()

    locals_ = [
        pltpu.make_async_copy(src, buf.at[own, c], local_sem.at[k])
        for k, (src, buf) in enumerate(((tok_in, tok), (grd_in, grd), (gat_in, gat)))
    ]
    weights = [
        pltpu.make_async_copy(src, dst, w_sem.at[k])
        for k, (src, dst) in enumerate(((wg_in, wg), (wu_in, wu), (wd_in, wd)))
    ]
    for copy in locals_ + weights:
        copy.start()

    barrier = pltpu.get_barrier_semaphore()

    def greet(d):
        pl.semaphore_signal(
            barrier, inc=1, device_id=nbr[d], device_id_type=pl.DeviceIdType.MESH
        )

    pl.when(z < LINE - 1)(lambda: greet(0))
    pl.when(z > 0)(lambda: greet(1))
    greet(2)
    greet(3)
    inside = (z + LINE - 1) // LINE * ((2 * LINE - 2 - z) // LINE)
    pl.semaphore_wait(barrier, 3 + inside)

    for copy in locals_:
        copy.wait()
    for k in (0, 2, 1):
        each_hop(k, z, start)
    down[...] = jnp.zeros_like(down)
    for copy in weights:
        copy.wait()

    def core_copy(u):
        return pltpu.make_async_remote_copy(
            src_ref=part.at[u, 1 - c],
            dst_ref=core_in.at[u],
            send_sem=a_send.at[u],
            recv_sem=a_recv.at[u],
            device_id=nbr[3],
            device_id_type=pl.DeviceIdType.MESH,
        )

    def y_copy(zu):
        return pltpu.make_async_remote_copy(
            src_ref=part.at[(1 - y) * LINE + zu, c],
            dst_ref=y_in.at[zu],
            send_sem=b_send.at[zu],
            recv_sem=b_recv.at[zu],
            device_id=nbr[2],
            device_id_type=pl.DeviceIdType.MESH,
        )

    def z_copy(zu, d):
        return pltpu.make_async_remote_copy(
            src_ref=part.at[y * LINE + zu, c],
            dst_ref=z_in.at[d, zu],
            send_sem=c_send.at[zu],
            recv_sem=c_recv.at[d, zu],
            device_id=nbr[d],
            device_id_type=pl.DeviceIdType.MESH,
        )

    def compute(u):
        rows, width, f = 2 * tok.shape[2], tok.shape[3], wg.shape[2]

        def expert(e, _):
            x = tok[u].reshape(rows, width)
            g = grd[u].reshape(rows, width)
            pg = jnp.dot(x, wg[e], preferred_element_type=jnp.float32)
            pu = jnp.dot(x, wu[e], preferred_element_type=jnp.float32)
            gh = lax.dot_general(
                g, wd[e], (((1,), (1,)), ((), ())), preferred_element_type=jnp.float32
            )
            row = me * wg.shape[0] + e
            cols = []
            for cc in range(2):
                line = gat[u, cc, pl.ds(row, 1), :]
                t = jnp.broadcast_to(line, (line.shape[1], line.shape[1])).T
                cols.append(jnp.concatenate([t] * (f // t.shape[1]), axis=1))
            gate = jnp.concatenate(cols, axis=0)
            sigma = jax.nn.sigmoid(pg)
            silu_val = pg * sigma
            hid[e] = (gate * (silu_val * pu)).T.astype(jnp.bfloat16)
            gh = gh * gate
            g_first[e] = (gh * pu * sigma * (1.0 + pg * (1.0 - sigma))).astype(jnp.bfloat16)
            g_second[e] = (gh * silu_val).astype(jnp.bfloat16)
            return 0

        lax.fori_loop(0, wg.shape[0], expert, 0)

        def columns(n, _):
            cs = pl.ds(pl.multiple_of(n * TILE, TILE), TILE)
            g = grd[u, :, :, cs].reshape(rows, TILE)
            total = None
            for e in range(wg.shape[0]):
                for a, w in ((g_first, wg), (g_second, wu)):
                    t = lax.dot_general(
                        a[e], w[e, cs, :], (((1,), (1,)), ((), ())),
                        preferred_element_type=jnp.float32,
                    )
                    total = t if total is None else total + t
                down[e, :, cs] += jnp.dot(hid[e], g, preferred_element_type=jnp.float32)
            half = rows // 2
            part[u, 0, :, cs] = total[:half].astype(jnp.bfloat16)
            part[u, 1, :, cs] = total[half:].astype(jnp.bfloat16)
            return 0

        lax.fori_loop(0, width // TILE, columns, 0)
        core_copy(u).start()

    def round_(r, _):
        for group in ((0, 2), (1,)):
            @pl.when((r > 0) & (r < LINE))
            def _():
                for k in group:
                    hop(k, y * LINE + place(r), c, 3).wait_recv()
                    each_hop(k, place(r), start)

            @pl.when(r > 0)
            def _():
                for k in group:
                    copy = hop(k, (1 - y) * LINE + place(r - 1), c, 3)
                    copy.wait_recv()
                    copy.start()

        def half(h, _):
            @pl.when((r - h >= 0) & (r - h < LINE))
            def _():
                u = (y + h * (1 - 2 * y)) * LINE + place(r - h)
                for k in range(3):
                    hop(k, u, 1 - c, 3).wait_recv()
                compute(u)
            return 0

        lax.fori_loop(0, 2, half, 0)
        return 0

    lax.fori_loop(0, LINE + 1, round_, 0)

    def send_y(j, _):
        zu = place(LINE - 1 - j)
        v = (1 - y) * LINE + zu
        core_copy(v).wait_recv()
        part[v, c] = (part[v, c].astype(jnp.float32) + core_in[v].astype(jnp.float32)).astype(
            jnp.bfloat16
        )
        y_copy(zu).start()
        return 0

    lax.fori_loop(0, LINE, send_y, 0)
    gd_out[...] = down[...].astype(gd_out.dtype)

    def send_z(j, _):
        zu = place(LINE - 1 - j)
        u = y * LINE + zu
        core_copy(u).wait_recv()
        acc[...] = part[u, c].astype(jnp.float32) + core_in[u].astype(jnp.float32)
        y_copy(zu).wait_recv()
        acc[...] += y_in[zu].astype(jnp.float32)

        @pl.when((zu >= z) & (z > 0))
        def _():
            z_copy(zu, 0).wait_recv()
            acc[...] += z_in[0, zu].astype(jnp.float32)

        @pl.when((zu <= z) & (z < LINE - 1))
        def _():
            z_copy(zu, 1).wait_recv()
            acc[...] += z_in[1, zu].astype(jnp.float32)

        @pl.when(zu == z)
        def _():
            gt_out[...] = acc[...].astype(gt_out.dtype)

        @pl.when(zu > z)
        def _():
            part[u, c] = acc[...].astype(jnp.bfloat16)
            z_copy(zu, 0).start()

        @pl.when(zu < z)
        def _():
            part[u, c] = acc[...].astype(jnp.bfloat16)
            z_copy(zu, 1).start()
        return 0

    lax.fori_loop(0, LINE, send_z, 0)

    def drain(zu, _):
        for k in range(3):
            each_hop(k, zu, done)
            hop(k, (1 - y) * LINE + zu, c, 3).wait_send()
        core_copy(zu).wait_send()
        core_copy(LINE + zu).wait_send()
        y_copy(zu).wait_send()
        pl.when(zu > z)(lambda: z_copy(zu, 0).wait_send())
        pl.when(zu < z)(lambda: z_copy(zu, 1).wait_send())
        return 0

    lax.fori_loop(0, LINE, drain, 0)


def fused_shards(tokens, grad_out, route_ids, gate_weights, w_gate, w_up, w_down):
    rows, width = tokens.shape
    local_experts, _, ff = w_gate.shape
    experts = local_experts * lax.axis_size("gx") * lax.axis_size("gy")
    units = 2 * LINE
    names = jnp.arange(experts, dtype=jnp.int32)[None, :, None]
    dense = jnp.sum(
        jnp.where(route_ids.T[:, None, :] == names, gate_weights.T[:, None, :], 0.0), axis=0
    )
    bf16, f32 = jnp.bfloat16, jnp.float32
    dma = pltpu.SemaphoreType.DMA
    return pl.pallas_call(
        fused_kernel,
        out_shape=(
            jax.ShapeDtypeStruct((rows, width), bf16),
            jax.ShapeDtypeStruct((local_experts, ff, width), bf16),
        ),
        in_specs=[pl.BlockSpec(memory_space=pl.ANY)] * 6,
        out_specs=[pl.BlockSpec(memory_space=pltpu.VMEM)] * 2,
        scratch_shapes=[
            pltpu.VMEM((units, 2, rows, width), bf16),
            pltpu.VMEM((units, 2, rows, width), bf16),
            pltpu.VMEM((units, 2, experts, rows), f32),
            pltpu.VMEM(w_gate.shape, bf16),
            pltpu.VMEM(w_up.shape, bf16),
            pltpu.VMEM(w_down.shape, bf16),
            pltpu.VMEM((units, 2, rows, width), bf16),
            pltpu.VMEM((units, rows, width), bf16),
            pltpu.VMEM((LINE, rows, width), bf16),
            pltpu.VMEM((2, LINE, rows, width), bf16),
            pltpu.VMEM((local_experts, ff, width), f32),
            pltpu.VMEM((local_experts, 2 * rows, ff), bf16),
            pltpu.VMEM((local_experts, 2 * rows, ff), bf16),
            pltpu.VMEM((local_experts, ff, 2 * rows), bf16),
            pltpu.VMEM((rows, width), f32),
            dma((3,)),
            dma((3,)),
            dma((3, units, 4)),
            dma((3, units, 2)),
            dma((units,)),
            dma((units,)),
            dma((LINE,)),
            dma((LINE,)),
            dma((LINE,)),
            dma((2, LINE)),
        ],
        compiler_params=pltpu.CompilerParams(
            collective_id=0, has_side_effects=True, vmem_limit_bytes=60 * 1024 * 1024
        ),
    )(tokens, grad_out, dense, w_gate, w_up, w_down)


def shards(*args):
    tokens, route_ids, w_gate = args[0], args[2], args[4]
    outer, inner = lax.axis_size("gx"), lax.axis_size("gy")
    experts = w_gate.shape[0] * outer * inner
    fits = tokens.shape[0] == 128 and w_gate.shape == (2, 2048, 256)
    if outer == 4 and inner == LINE and fits and experts <= 4 * route_ids.shape[1]:
        return fused_shards(*args)
    return routed_shards(*args)


def solution(mesh):
    placed = (
        P(("rep", "gx", "gy"), None),
        P(("rep", "gx", "gy"), None),
        P(("rep", "gx", "gy"), None),
        P(("rep", "gx", "gy"), None),
        P(("gx", "gy"), None, None),
        P(("gx", "gy"), None, None),
        P(("gx", "gy"), None, None),
    )
    return jax.shard_map(
        shards,
        mesh=mesh,
        in_specs=placed,
        out_specs=(P(("rep", "gx", "gy"), None), P(("rep", "gx", "gy"), None, None)),
        check_vma=False,
    )
```

```python
import jax
import jax.numpy as jnp
from jax import lax
from jax.experimental import pallas as pl
from jax.experimental.pallas import tpu as pltpu
from jax.sharding import PartitionSpec as P


LINE = 4
TILE = 512
PARTS = 2


def routed_shards(tokens, grad_out, route_ids, gate_weights, w_gate, w_up, w_down):
    token_count = tokens.shape[0]
    model_width = tokens.shape[1]
    fanout = route_ids.shape[1]
    local_experts = w_gate.shape[0]
    outer_size = lax.axis_size("gx")
    inner_size = lax.axis_size("gy")
    devices = outer_size * inner_size
    experts = local_experts * devices
    capacity = max(2, 5 * token_count * fanout // (4 * experts))
    flat_ids = route_ids.reshape(-1)
    onehot = (flat_ids[:, None] == jnp.arange(experts, dtype=jnp.int32)[None, :]).astype(jnp.int32)
    earlier = jnp.cumsum(onehot, axis=0) - onehot
    slot_index = jnp.sum(earlier * onehot, axis=1)
    target = flat_ids // local_experts
    within = flat_ids % local_experts
    position = (within * devices + target) * capacity + slot_index
    source_rows = jnp.repeat(tokens, fanout, axis=0)
    scaled = (gate_weights.reshape(-1, 1) * jnp.repeat(grad_out, fanout, axis=0)).astype(
        jnp.bfloat16
    )
    buffer_rows = local_experts * devices * capacity
    send_inputs = jnp.zeros((buffer_rows, model_width), jnp.bfloat16).at[position].set(source_rows)
    send_grads = jnp.zeros((buffer_rows, model_width), jnp.bfloat16).at[position].set(scaled)
    flat_shape = (local_experts, devices, capacity, model_width)
    got_inputs, got_grads = (
        lax.all_to_all(
            send_inputs.reshape(flat_shape), ("gx", "gy"), split_axis=1, concat_axis=1, tiled=True
        ),
        lax.all_to_all(
            send_grads.reshape(flat_shape), ("gx", "gy"), split_axis=1, concat_axis=1, tiled=True
        ),
    )
    expert_rows = devices * capacity
    inputs = got_inputs.reshape(local_experts, expert_rows, model_width)
    routed = got_grads.reshape(local_experts, expert_rows, model_width)
    pre_gate = jnp.einsum("emd,edf->emf", inputs, w_gate, preferred_element_type=jnp.float32)
    pre_up = jnp.einsum("emd,edf->emf", inputs, w_up, preferred_element_type=jnp.float32)
    sigma = jax.nn.sigmoid(pre_gate)
    silu_val = pre_gate * sigma
    hidden = (silu_val * pre_up).astype(jnp.bfloat16)
    grad_hidden = jnp.einsum("emd,efd->emf", routed, w_down, preferred_element_type=jnp.float32)
    grad_first = (grad_hidden * pre_up * sigma * (1.0 + pre_gate * (1.0 - sigma))).astype(
        jnp.bfloat16
    )
    grad_second = (grad_hidden * silu_val).astype(jnp.bfloat16)
    grad_route = (
        jnp.einsum("emf,edf->emd", grad_first, w_gate, preferred_element_type=jnp.float32)
        + jnp.einsum("emf,edf->emd", grad_second, w_up, preferred_element_type=jnp.float32)
    ).astype(jnp.bfloat16)
    grad_down = jnp.einsum(
        "emf,emd->efd", hidden, routed, preferred_element_type=jnp.float32
    ).astype(jnp.bfloat16)
    returned = lax.all_to_all(
        grad_route.reshape(flat_shape), ("gx", "gy"), split_axis=1, concat_axis=1, tiled=True
    )
    picked = returned.reshape(buffer_rows, model_width)[position]
    grad_tokens = jnp.sum(
        picked.astype(jnp.float32).reshape(token_count, fanout, model_width), axis=1
    ).astype(jnp.bfloat16)
    return (grad_tokens, grad_down)


def fused_kernel(
    tok_in, grd_in, gat_in, wg_in, wu_in, wd_in, gt_out, gd_out,
    tok, grd, gat, wg, wu, wd, part, core_in, y_in, z_in, down, g_first, g_second, hid, acc,
    local_sem, w_sem, send_sem, recv_sem, a_send, a_recv, b_send, b_recv, c_send, c_recv,
):
    gx, z = lax.axis_index("gx"), lax.axis_index("gy")
    y, c = gx // 2, gx % 2
    me = gx * LINE + z
    nbr = (
        {"gx": gx, "gy": z + 1},
        {"gx": gx, "gy": z - 1},
        {"gx": (1 - y) * 2 + c, "gy": z},
        {"gx": y * 2 + 1 - c, "gy": z},
    )
    rows = tok.shape[2]
    kinds = 1 + 2 * PARTS
    half_rows = rows // 2
    own = y * LINE + z
    high = z // 2
    edge = z + high * (3 - 2 * z)

    def place(r):
        o = r + edge * (1 - r // 2) * (1 - 2 * (r % 2))
        return o + high * (3 - 2 * o)

    def piece(k, u, cc):
        if k == 0:
            return gat.at[u, cc]
        size = rows // PARTS
        return (tok, grd)[(k - 1) // PARTS].at[u, cc, pl.ds((k - 1) % PARTS * size, size)]

    def hop(k, u, cc, d):
        return pltpu.make_async_remote_copy(
            src_ref=piece(k, u, cc),
            dst_ref=piece(k, u, cc),
            send_sem=send_sem.at[k, u, d],
            recv_sem=recv_sem.at[k, u, cc],
            device_id=nbr[d],
            device_id_type=pl.DeviceIdType.MESH,
        )

    def each_hop(k, zu, act):
        u = y * LINE + zu

        @pl.when((zu <= z) & (z < LINE - 1))
        def _():
            act(hop(k, u, c, 0))

        @pl.when((zu >= z) & (z > 0))
        def _():
            act(hop(k, u, c, 1))

        act(hop(k, u, c, 2))
        act(hop(k, u, c, 3))

    def start(copy):
        copy.start()

    def done(copy):
        copy.wait_send()

    locals_ = [
        pltpu.make_async_copy(src, buf.at[own, c], local_sem.at[k])
        for k, (src, buf) in enumerate(((tok_in, tok), (grd_in, grd), (gat_in, gat)))
    ]
    weights = [
        pltpu.make_async_copy(src, dst, w_sem.at[k])
        for k, (src, dst) in enumerate(((wg_in, wg), (wu_in, wu), (wd_in, wd)))
    ]
    for copy in locals_ + weights:
        copy.start()

    barrier = pltpu.get_barrier_semaphore()

    def greet(d):
        pl.semaphore_signal(
            barrier, inc=1, device_id=nbr[d], device_id_type=pl.DeviceIdType.MESH
        )

    pl.when(z < LINE - 1)(lambda: greet(0))
    pl.when(z > 0)(lambda: greet(1))
    greet(2)
    greet(3)
    inside = (z + LINE - 1) // LINE * ((2 * LINE - 2 - z) // LINE)
    pl.semaphore_wait(barrier, 3 + inside)

    for copy in locals_:
        copy.wait()
    for k in range(kinds):
        each_hop(k, z, start)
    down[...] = jnp.zeros_like(down)
    for copy in weights:
        copy.wait()

    def core_copy(u):
        return pltpu.make_async_remote_copy(
            src_ref=part.at[u, 1 - c],
            dst_ref=core_in.at[u],
            send_sem=a_send.at[u],
            recv_sem=a_recv.at[u],
            device_id=nbr[3],
            device_id_type=pl.DeviceIdType.MESH,
        )

    def span(h):
        return pl.ds(pl.multiple_of(h * half_rows, half_rows), half_rows)

    def y_copy(zu, h):
        return pltpu.make_async_remote_copy(
            src_ref=part.at[(1 - y) * LINE + zu, c, span(h)],
            dst_ref=y_in.at[zu, span(h)],
            send_sem=b_send.at[zu, h],
            recv_sem=b_recv.at[zu, h],
            device_id=nbr[2],
            device_id_type=pl.DeviceIdType.MESH,
        )

    def z_copy(zu, h, d):
        return pltpu.make_async_remote_copy(
            src_ref=part.at[y * LINE + zu, c, span(h)],
            dst_ref=z_in.at[d, zu, span(h)],
            send_sem=c_send.at[zu, h],
            recv_sem=c_recv.at[d, zu, h],
            device_id=nbr[d],
            device_id_type=pl.DeviceIdType.MESH,
        )

    def compute(u):
        rows, width, f = 2 * tok.shape[2], tok.shape[3], wg.shape[2]

        def expert(e, _):
            x = tok[u].reshape(rows, width)
            g = grd[u].reshape(rows, width)
            pg = jnp.dot(x, wg[e], preferred_element_type=jnp.float32)
            pu = jnp.dot(x, wu[e], preferred_element_type=jnp.float32)
            gh = lax.dot_general(
                g, wd[e], (((1,), (1,)), ((), ())), preferred_element_type=jnp.float32
            )
            row = me * wg.shape[0] + e
            cols = []
            for cc in range(2):
                line = gat[u, cc, pl.ds(row, 1), :]
                t = jnp.broadcast_to(line, (line.shape[1], line.shape[1])).T
                cols.append(jnp.concatenate([t] * (f // t.shape[1]), axis=1))
            gate = jnp.concatenate(cols, axis=0)
            sigma = jax.nn.sigmoid(pg)
            silu_val = pg * sigma
            hid[e] = (gate * (silu_val * pu)).T.astype(jnp.bfloat16)
            gh = gh * gate
            g_first[e] = (gh * pu * sigma * (1.0 + pg * (1.0 - sigma))).astype(jnp.bfloat16)
            g_second[e] = (gh * silu_val).astype(jnp.bfloat16)
            return 0

        lax.fori_loop(0, wg.shape[0], expert, 0)

        def columns(n, _):
            cs = pl.ds(pl.multiple_of(n * TILE, TILE), TILE)
            g = grd[u, :, :, cs].reshape(rows, TILE)
            total = None
            for e in range(wg.shape[0]):
                for a, w in ((g_first, wg), (g_second, wu)):
                    t = lax.dot_general(
                        a[e], w[e, cs, :], (((1,), (1,)), ((), ())),
                        preferred_element_type=jnp.float32,
                    )
                    total = t if total is None else total + t
                down[e, :, cs] += jnp.dot(hid[e], g, preferred_element_type=jnp.float32)
            half = rows // 2
            part[u, 0, :, cs] = total[:half].astype(jnp.bfloat16)
            part[u, 1, :, cs] = total[half:].astype(jnp.bfloat16)
            return 0

        lax.fori_loop(0, width // TILE, columns, 0)
        core_copy(u).start()

    def turn(j):
        return place((1 - j // 2) * (2 + j) + j // 2 * (3 - j))

    def send_y(j, _):
        zu = turn(j)
        v = (1 - y) * LINE + zu
        core_copy(v).wait_recv()

        def one(h, _):
            part[v, c, span(h)] = (
                part[v, c, span(h)].astype(jnp.float32)
                + core_in[v, span(h)].astype(jnp.float32)
            ).astype(jnp.bfloat16)
            y_copy(zu, h).start()
            return 0

        lax.fori_loop(0, 2, one, 0)
        return 0

    def round_(r, _):
        for k in range(kinds):
            @pl.when((r > 0) & (r < LINE))
            def _():
                hop(k, y * LINE + place(r), c, 3).wait_recv()
                each_hop(k, place(r), start)

            @pl.when(r > 0)
            def _():
                copy = hop(k, (1 - y) * LINE + place(r - 1), c, 3)
                copy.wait_recv()
                copy.start()

        @pl.when(r == LINE)
        def _():
            send_y(0, 0)

        def half(h, _):
            @pl.when((r - h >= 0) & (r - h < LINE))
            def _():
                u = (y + h * (1 - 2 * y)) * LINE + place(r - h)
                for k in range(kinds):
                    hop(k, u, 1 - c, 3).wait_recv()
                compute(u)
            return 0

        lax.fori_loop(0, 2, half, 0)
        return 0

    lax.fori_loop(0, LINE + 1, round_, 0)

    lax.fori_loop(1, LINE, send_y, 0)
    gd_out[...] = down[...].astype(gd_out.dtype)

    def send_z(i, _):
        zu, h = turn(i // 2), i % 2
        u = y * LINE + zu

        @pl.when(h == 0)
        def _():
            core_copy(u).wait_recv()

        acc[...] = part[u, c, span(h)].astype(jnp.float32) + core_in[u, span(h)].astype(
            jnp.float32
        )
        y_copy(zu, h).wait_recv()
        acc[...] += y_in[zu, span(h)].astype(jnp.float32)

        @pl.when((zu >= z) & (z > 0))
        def _():
            z_copy(zu, h, 0).wait_recv()
            acc[...] += z_in[0, zu, span(h)].astype(jnp.float32)

        @pl.when((zu <= z) & (z < LINE - 1))
        def _():
            z_copy(zu, h, 1).wait_recv()
            acc[...] += z_in[1, zu, span(h)].astype(jnp.float32)

        @pl.when(zu == z)
        def _():
            gt_out[span(h)] = acc[...].astype(gt_out.dtype)

        @pl.when(zu > z)
        def _():
            part[u, c, span(h)] = acc[...].astype(jnp.bfloat16)
            z_copy(zu, h, 0).start()

        @pl.when(zu < z)
        def _():
            part[u, c, span(h)] = acc[...].astype(jnp.bfloat16)
            z_copy(zu, h, 1).start()
        return 0

    lax.fori_loop(0, 2 * LINE, send_z, 0)

    def drain(zu, _):
        for k in range(kinds):
            each_hop(k, zu, done)
            hop(k, (1 - y) * LINE + zu, c, 3).wait_send()
        core_copy(zu).wait_send()
        core_copy(LINE + zu).wait_send()
        for h in range(2):
            y_copy(zu, h).wait_send()
            pl.when(zu > z)(lambda: z_copy(zu, h, 0).wait_send())
            pl.when(zu < z)(lambda: z_copy(zu, h, 1).wait_send())
        return 0

    lax.fori_loop(0, LINE, drain, 0)


def fused_shards(tokens, grad_out, route_ids, gate_weights, w_gate, w_up, w_down):
    rows, width = tokens.shape
    local_experts, _, ff = w_gate.shape
    experts = local_experts * lax.axis_size("gx") * lax.axis_size("gy")
    units = 2 * LINE
    names = jnp.arange(experts, dtype=jnp.int32)[None, :, None]
    dense = jnp.sum(
        jnp.where(route_ids.T[:, None, :] == names, gate_weights.T[:, None, :], 0.0), axis=0
    )
    bf16, f32 = jnp.bfloat16, jnp.float32
    dma = pltpu.SemaphoreType.DMA
    return pl.pallas_call(
        fused_kernel,
        out_shape=(
            jax.ShapeDtypeStruct((rows, width), bf16),
            jax.ShapeDtypeStruct((local_experts, ff, width), bf16),
        ),
        in_specs=[pl.BlockSpec(memory_space=pl.ANY)] * 6,
        out_specs=[pl.BlockSpec(memory_space=pltpu.VMEM)] * 2,
        scratch_shapes=[
            pltpu.VMEM((units, 2, rows, width), bf16),
            pltpu.VMEM((units, 2, rows, width), bf16),
            pltpu.VMEM((units, 2, experts, rows), f32),
            pltpu.VMEM(w_gate.shape, bf16),
            pltpu.VMEM(w_up.shape, bf16),
            pltpu.VMEM(w_down.shape, bf16),
            pltpu.VMEM((units, 2, rows, width), bf16),
            pltpu.VMEM((units, rows, width), bf16),
            pltpu.VMEM((LINE, rows, width), bf16),
            pltpu.VMEM((2, LINE, rows, width), bf16),
            pltpu.VMEM((local_experts, ff, width), f32),
            pltpu.VMEM((local_experts, 2 * rows, ff), bf16),
            pltpu.VMEM((local_experts, 2 * rows, ff), bf16),
            pltpu.VMEM((local_experts, ff, 2 * rows), bf16),
            pltpu.VMEM((rows // 2, width), f32),
            dma((3,)),
            dma((3,)),
            dma((1 + 2 * PARTS, units, 4)),
            dma((1 + 2 * PARTS, units, 2)),
            dma((units,)),
            dma((units,)),
            dma((LINE, 2)),
            dma((LINE, 2)),
            dma((LINE, 2)),
            dma((2, LINE, 2)),
        ],
        compiler_params=pltpu.CompilerParams(
            collective_id=0, has_side_effects=True, vmem_limit_bytes=60 * 1024 * 1024
        ),
    )(tokens, grad_out, dense, w_gate, w_up, w_down)


def shards(*args):
    tokens, route_ids, w_gate = args[0], args[2], args[4]
    outer, inner = lax.axis_size("gx"), lax.axis_size("gy")
    experts = w_gate.shape[0] * outer * inner
    fits = tokens.shape[0] == 128 and w_gate.shape == (2, 2048, 256)
    if outer == 4 and inner == LINE and fits and experts <= 4 * route_ids.shape[1]:
        return fused_shards(*args)
    return routed_shards(*args)


def solution(mesh):
    placed = (
        P(("rep", "gx", "gy"), None),
        P(("rep", "gx", "gy"), None),
        P(("rep", "gx", "gy"), None),
        P(("rep", "gx", "gy"), None),
        P(("gx", "gy"), None, None),
        P(("gx", "gy"), None, None),
        P(("gx", "gy"), None, None),
    )
    return jax.shard_map(
        shards,
        mesh=mesh,
        in_specs=placed,
        out_specs=(P(("rep", "gx", "gy"), None), P(("rep", "gx", "gy"), None, None)),
        check_vma=False,
    )
```

```python
import jax
import jax.numpy as jnp
from jax import lax
from jax.experimental import pallas as pl
from jax.experimental.pallas import tpu as pltpu
from jax.sharding import PartitionSpec as P


LINE = 4
TILE = 512
PARTS = 2
SUMS = 4


def routed_shards(tokens, grad_out, route_ids, gate_weights, w_gate, w_up, w_down):
    token_count = tokens.shape[0]
    model_width = tokens.shape[1]
    fanout = route_ids.shape[1]
    local_experts = w_gate.shape[0]
    outer_size = lax.axis_size("gx")
    inner_size = lax.axis_size("gy")
    devices = outer_size * inner_size
    experts = local_experts * devices
    capacity = max(2, 5 * token_count * fanout // (4 * experts))
    flat_ids = route_ids.reshape(-1)
    onehot = (flat_ids[:, None] == jnp.arange(experts, dtype=jnp.int32)[None, :]).astype(jnp.int32)
    earlier = jnp.cumsum(onehot, axis=0) - onehot
    slot_index = jnp.sum(earlier * onehot, axis=1)
    target = flat_ids // local_experts
    within = flat_ids % local_experts
    position = (within * devices + target) * capacity + slot_index
    source_rows = jnp.repeat(tokens, fanout, axis=0)
    scaled = (gate_weights.reshape(-1, 1) * jnp.repeat(grad_out, fanout, axis=0)).astype(
        jnp.bfloat16
    )
    buffer_rows = local_experts * devices * capacity
    send_inputs = jnp.zeros((buffer_rows, model_width), jnp.bfloat16).at[position].set(source_rows)
    send_grads = jnp.zeros((buffer_rows, model_width), jnp.bfloat16).at[position].set(scaled)
    flat_shape = (local_experts, devices, capacity, model_width)
    got_inputs, got_grads = (
        lax.all_to_all(
            send_inputs.reshape(flat_shape), ("gx", "gy"), split_axis=1, concat_axis=1, tiled=True
        ),
        lax.all_to_all(
            send_grads.reshape(flat_shape), ("gx", "gy"), split_axis=1, concat_axis=1, tiled=True
        ),
    )
    expert_rows = devices * capacity
    inputs = got_inputs.reshape(local_experts, expert_rows, model_width)
    routed = got_grads.reshape(local_experts, expert_rows, model_width)
    pre_gate = jnp.einsum("emd,edf->emf", inputs, w_gate, preferred_element_type=jnp.float32)
    pre_up = jnp.einsum("emd,edf->emf", inputs, w_up, preferred_element_type=jnp.float32)
    sigma = jax.nn.sigmoid(pre_gate)
    silu_val = pre_gate * sigma
    hidden = (silu_val * pre_up).astype(jnp.bfloat16)
    grad_hidden = jnp.einsum("emd,efd->emf", routed, w_down, preferred_element_type=jnp.float32)
    grad_first = (grad_hidden * pre_up * sigma * (1.0 + pre_gate * (1.0 - sigma))).astype(
        jnp.bfloat16
    )
    grad_second = (grad_hidden * silu_val).astype(jnp.bfloat16)
    grad_route = (
        jnp.einsum("emf,edf->emd", grad_first, w_gate, preferred_element_type=jnp.float32)
        + jnp.einsum("emf,edf->emd", grad_second, w_up, preferred_element_type=jnp.float32)
    ).astype(jnp.bfloat16)
    grad_down = jnp.einsum(
        "emf,emd->efd", hidden, routed, preferred_element_type=jnp.float32
    ).astype(jnp.bfloat16)
    returned = lax.all_to_all(
        grad_route.reshape(flat_shape), ("gx", "gy"), split_axis=1, concat_axis=1, tiled=True
    )
    picked = returned.reshape(buffer_rows, model_width)[position]
    grad_tokens = jnp.sum(
        picked.astype(jnp.float32).reshape(token_count, fanout, model_width), axis=1
    ).astype(jnp.bfloat16)
    return (grad_tokens, grad_down)


def fused_kernel(
    tok_in, grd_in, gat_in, wg_in, wu_in, wd_in, gt_out, gd_out,
    tok, grd, gat, wg, wu, wd, part, core_in, y_in, z_in, down, g_first, g_second, hid, acc,
    local_sem, w_sem, send_sem, recv_sem, a_send, a_recv, b_send, b_recv, c_send, c_recv,
):
    gx, z = lax.axis_index("gx"), lax.axis_index("gy")
    y, c = gx // 2, gx % 2
    me = gx * LINE + z
    nbr = (
        {"gx": gx, "gy": z + 1},
        {"gx": gx, "gy": z - 1},
        {"gx": (1 - y) * 2 + c, "gy": z},
        {"gx": y * 2 + 1 - c, "gy": z},
    )
    rows = tok.shape[2]
    kinds = 1 + 2 * PARTS
    half_rows = rows // SUMS
    own = y * LINE + z
    high = z // 2
    edge = z + high * (3 - 2 * z)

    def place(r):
        o = r + edge * (1 - r // 2) * (1 - 2 * (r % 2))
        return o + high * (3 - 2 * o)

    def piece(k, u, cc):
        if k == 0:
            return gat.at[u, cc]
        size = rows // PARTS
        return (tok, grd)[(k - 1) // PARTS].at[u, cc, pl.ds((k - 1) % PARTS * size, size)]

    def hop(k, u, cc, d):
        return pltpu.make_async_remote_copy(
            src_ref=piece(k, u, cc),
            dst_ref=piece(k, u, cc),
            send_sem=send_sem.at[k, u, d],
            recv_sem=recv_sem.at[k, u, cc],
            device_id=nbr[d],
            device_id_type=pl.DeviceIdType.MESH,
        )

    def each_hop(k, zu, act):
        u = y * LINE + zu

        @pl.when((zu <= z) & (z < LINE - 1))
        def _():
            act(hop(k, u, c, 0))

        @pl.when((zu >= z) & (z > 0))
        def _():
            act(hop(k, u, c, 1))

        act(hop(k, u, c, 2))
        act(hop(k, u, c, 3))

    def start(copy):
        copy.start()

    def done(copy):
        copy.wait_send()

    locals_ = [
        pltpu.make_async_copy(src, buf.at[own, c], local_sem.at[k])
        for k, (src, buf) in enumerate(((tok_in, tok), (grd_in, grd), (gat_in, gat)))
    ]
    weights = [
        pltpu.make_async_copy(src, dst, w_sem.at[k])
        for k, (src, dst) in enumerate(((wg_in, wg), (wu_in, wu), (wd_in, wd)))
    ]
    for copy in locals_ + weights:
        copy.start()

    barrier = pltpu.get_barrier_semaphore()

    def greet(d):
        pl.semaphore_signal(
            barrier, inc=1, device_id=nbr[d], device_id_type=pl.DeviceIdType.MESH
        )

    pl.when(z < LINE - 1)(lambda: greet(0))
    pl.when(z > 0)(lambda: greet(1))
    greet(2)
    greet(3)
    inside = (z + LINE - 1) // LINE * ((2 * LINE - 2 - z) // LINE)
    pl.semaphore_wait(barrier, 3 + inside)

    for copy in locals_:
        copy.wait()
    for k in range(kinds):
        each_hop(k, z, start)
    down[...] = jnp.zeros_like(down)
    for copy in weights:
        copy.wait()

    def core_copy(u):
        return pltpu.make_async_remote_copy(
            src_ref=part.at[u, 1 - c],
            dst_ref=core_in.at[u],
            send_sem=a_send.at[u],
            recv_sem=a_recv.at[u],
            device_id=nbr[3],
            device_id_type=pl.DeviceIdType.MESH,
        )

    def span(h):
        return pl.ds(pl.multiple_of(h * half_rows, half_rows), half_rows)

    def y_copy(zu, h):
        return pltpu.make_async_remote_copy(
            src_ref=part.at[(1 - y) * LINE + zu, c, span(h)],
            dst_ref=y_in.at[zu, span(h)],
            send_sem=b_send.at[zu, h],
            recv_sem=b_recv.at[zu, h],
            device_id=nbr[2],
            device_id_type=pl.DeviceIdType.MESH,
        )

    def z_copy(zu, h, d):
        return pltpu.make_async_remote_copy(
            src_ref=part.at[y * LINE + zu, c, span(h)],
            dst_ref=z_in.at[d, zu, span(h)],
            send_sem=c_send.at[zu, h],
            recv_sem=c_recv.at[d, zu, h],
            device_id=nbr[d],
            device_id_type=pl.DeviceIdType.MESH,
        )

    def compute(u):
        rows, width, f = 2 * tok.shape[2], tok.shape[3], wg.shape[2]

        def expert(e, _):
            x = tok[u].reshape(rows, width)
            g = grd[u].reshape(rows, width)
            pg = jnp.dot(x, wg[e], preferred_element_type=jnp.float32)
            pu = jnp.dot(x, wu[e], preferred_element_type=jnp.float32)
            gh = lax.dot_general(
                g, wd[e], (((1,), (1,)), ((), ())), preferred_element_type=jnp.float32
            )
            row = me * wg.shape[0] + e
            cols = []
            for cc in range(2):
                line = gat[u, cc, pl.ds(row, 1), :]
                t = jnp.broadcast_to(line, (line.shape[1], line.shape[1])).T
                cols.append(jnp.concatenate([t] * (f // t.shape[1]), axis=1))
            gate = jnp.concatenate(cols, axis=0)
            sigma = jax.nn.sigmoid(pg)
            silu_val = pg * sigma
            hid[e] = (gate * (silu_val * pu)).T.astype(jnp.bfloat16)
            gh = gh * gate
            g_first[e] = (gh * pu * sigma * (1.0 + pg * (1.0 - sigma))).astype(jnp.bfloat16)
            g_second[e] = (gh * silu_val).astype(jnp.bfloat16)
            return 0

        lax.fori_loop(0, wg.shape[0], expert, 0)

        def columns(n, _):
            cs = pl.ds(pl.multiple_of(n * TILE, TILE), TILE)
            g = grd[u, :, :, cs].reshape(rows, TILE)
            total = None
            for e in range(wg.shape[0]):
                for a, w in ((g_first, wg), (g_second, wu)):
                    t = lax.dot_general(
                        a[e], w[e, cs, :], (((1,), (1,)), ((), ())),
                        preferred_element_type=jnp.float32,
                    )
                    total = t if total is None else total + t
                down[e, :, cs] += jnp.dot(hid[e], g, preferred_element_type=jnp.float32)
            half = rows // 2
            part[u, 0, :, cs] = total[:half].astype(jnp.bfloat16)
            part[u, 1, :, cs] = total[half:].astype(jnp.bfloat16)
            return 0

        lax.fori_loop(0, width // TILE, columns, 0)
        core_copy(u).start()

    def turn(j):
        return place((1 - j // 2) * (2 + j) + j // 2 * (3 - j))

    def send_y(j, _):
        zu = turn(j)
        v = (1 - y) * LINE + zu
        core_copy(v).wait_recv()

        def one(h, _):
            part[v, c, span(h)] = (
                part[v, c, span(h)].astype(jnp.float32)
                + core_in[v, span(h)].astype(jnp.float32)
            ).astype(jnp.bfloat16)
            y_copy(zu, h).start()
            return 0

        lax.fori_loop(0, SUMS, one, 0)
        return 0

    def round_(r, _):
        for k in range(kinds):
            @pl.when((r > 0) & (r < LINE))
            def _():
                hop(k, y * LINE + place(r), c, 3).wait_recv()
                each_hop(k, place(r), start)

            @pl.when(r > 0)
            def _():
                copy = hop(k, (1 - y) * LINE + place(r - 1), c, 3)
                copy.wait_recv()
                copy.start()

        @pl.when(r == LINE)
        def _():
            send_y(0, 0)

        def half(h, _):
            @pl.when((r - h >= 0) & (r - h < LINE))
            def _():
                u = (y + h * (1 - 2 * y)) * LINE + place(r - h)
                for k in range(kinds):
                    hop(k, u, 1 - c, 3).wait_recv()
                compute(u)
            return 0

        lax.fori_loop(0, 2, half, 0)
        return 0

    lax.fori_loop(0, LINE + 1, round_, 0)

    lax.fori_loop(1, LINE, send_y, 0)
    gd_out[...] = down[...].astype(gd_out.dtype)

    def send_z(i, _):
        zu, h = turn(i // SUMS), i % SUMS
        u = y * LINE + zu

        @pl.when(h == 0)
        def _():
            core_copy(u).wait_recv()

        acc[...] = part[u, c, span(h)].astype(jnp.float32) + core_in[u, span(h)].astype(
            jnp.float32
        )
        y_copy(zu, h).wait_recv()
        acc[...] += y_in[zu, span(h)].astype(jnp.float32)

        @pl.when((zu >= z) & (z > 0))
        def _():
            z_copy(zu, h, 0).wait_recv()
            acc[...] += z_in[0, zu, span(h)].astype(jnp.float32)

        @pl.when((zu <= z) & (z < LINE - 1))
        def _():
            z_copy(zu, h, 1).wait_recv()
            acc[...] += z_in[1, zu, span(h)].astype(jnp.float32)

        @pl.when(zu == z)
        def _():
            gt_out[span(h)] = acc[...].astype(gt_out.dtype)

        @pl.when(zu > z)
        def _():
            part[u, c, span(h)] = acc[...].astype(jnp.bfloat16)
            z_copy(zu, h, 0).start()

        @pl.when(zu < z)
        def _():
            part[u, c, span(h)] = acc[...].astype(jnp.bfloat16)
            z_copy(zu, h, 1).start()
        return 0

    lax.fori_loop(0, SUMS * LINE, send_z, 0)

    def drain(zu, _):
        for k in range(kinds):
            each_hop(k, zu, done)
            hop(k, (1 - y) * LINE + zu, c, 3).wait_send()
        core_copy(zu).wait_send()
        core_copy(LINE + zu).wait_send()
        for h in range(SUMS):
            y_copy(zu, h).wait_send()
            pl.when(zu > z)(lambda: z_copy(zu, h, 0).wait_send())
            pl.when(zu < z)(lambda: z_copy(zu, h, 1).wait_send())
        return 0

    lax.fori_loop(0, LINE, drain, 0)


def fused_shards(tokens, grad_out, route_ids, gate_weights, w_gate, w_up, w_down):
    rows, width = tokens.shape
    local_experts, _, ff = w_gate.shape
    experts = local_experts * lax.axis_size("gx") * lax.axis_size("gy")
    units = 2 * LINE
    names = jnp.arange(experts, dtype=jnp.int32)[None, :, None]
    dense = jnp.sum(
        jnp.where(route_ids.T[:, None, :] == names, gate_weights.T[:, None, :], 0.0), axis=0
    )
    bf16, f32 = jnp.bfloat16, jnp.float32
    dma = pltpu.SemaphoreType.DMA
    return pl.pallas_call(
        fused_kernel,
        out_shape=(
            jax.ShapeDtypeStruct((rows, width), bf16),
            jax.ShapeDtypeStruct((local_experts, ff, width), bf16),
        ),
        in_specs=[pl.BlockSpec(memory_space=pl.ANY)] * 6,
        out_specs=[pl.BlockSpec(memory_space=pltpu.VMEM)] * 2,
        scratch_shapes=[
            pltpu.VMEM((units, 2, rows, width), bf16),
            pltpu.VMEM((units, 2, rows, width), bf16),
            pltpu.VMEM((units, 2, experts, rows), f32),
            pltpu.VMEM(w_gate.shape, bf16),
            pltpu.VMEM(w_up.shape, bf16),
            pltpu.VMEM(w_down.shape, bf16),
            pltpu.VMEM((units, 2, rows, width), bf16),
            pltpu.VMEM((units, rows, width), bf16),
            pltpu.VMEM((LINE, rows, width), bf16),
            pltpu.VMEM((2, LINE, rows, width), bf16),
            pltpu.VMEM((local_experts, ff, width), f32),
            pltpu.VMEM((local_experts, 2 * rows, ff), bf16),
            pltpu.VMEM((local_experts, 2 * rows, ff), bf16),
            pltpu.VMEM((local_experts, ff, 2 * rows), bf16),
            pltpu.VMEM((rows // SUMS, width), f32),
            dma((3,)),
            dma((3,)),
            dma((1 + 2 * PARTS, units, 4)),
            dma((1 + 2 * PARTS, units, 2)),
            dma((units,)),
            dma((units,)),
            dma((LINE, SUMS)),
            dma((LINE, SUMS)),
            dma((LINE, SUMS)),
            dma((2, LINE, SUMS)),
        ],
        compiler_params=pltpu.CompilerParams(
            collective_id=0, has_side_effects=True, vmem_limit_bytes=60 * 1024 * 1024
        ),
    )(tokens, grad_out, dense, w_gate, w_up, w_down)


def shards(*args):
    tokens, route_ids, w_gate = args[0], args[2], args[4]
    outer, inner = lax.axis_size("gx"), lax.axis_size("gy")
    experts = w_gate.shape[0] * outer * inner
    fits = tokens.shape[0] == 128 and w_gate.shape == (2, 2048, 256)
    if outer == 4 and inner == LINE and fits and experts <= 4 * route_ids.shape[1]:
        return fused_shards(*args)
    return routed_shards(*args)


def solution(mesh):
    placed = (
        P(("rep", "gx", "gy"), None),
        P(("rep", "gx", "gy"), None),
        P(("rep", "gx", "gy"), None),
        P(("rep", "gx", "gy"), None),
        P(("gx", "gy"), None, None),
        P(("gx", "gy"), None, None),
        P(("gx", "gy"), None, None),
    )
    return jax.shard_map(
        shards,
        mesh=mesh,
        in_specs=placed,
        out_specs=(P(("rep", "gx", "gy"), None), P(("rep", "gx", "gy"), None, None)),
        check_vma=False,
    )
```
